32 devices in a mesh: groups: 2 (over x), ranks: 8 (over z, y), tensor: 2 (over core).
Axes of the slice: x: 2, y: 2, z: 4, core: 2. Of those that a mesh axis runs over, the one named last changes fastest.
Arguments:
- hidden: bfloat16 [2048, 7168], P(('groups', 'ranks'), 'tensor'), parts along dimension 0, may hold values from -6 to 6
- w_down: bfloat16 [7168, 576], P('tensor'), may hold values from -0.0625 to 0.0625
- latent_gain: bfloat16 [512], replicated, may hold values from 0.099609375 to 1.8984375
- queries: bfloat16 [2048, 36864], P(('groups', 'ranks'), 'tensor'), parts along dimension 0, may hold values from -100 to 100
- w_up_value: bfloat16 [64, 512, 128], P('tensor', 'ranks'), may hold values from -0.25 to 0.25
- prompt_blocks: int32 [8], P('groups'), parts along dimension 0, may hold values from 1 to 4, 8 in all
- migrate: int32 [16, 8], P('groups'), parts along dimension 0, may hold values from 0 to 7, as said below
- owners: int32 [16, 8], P('groups'), parts along dimension 0, may hold values from 0 to 7, as said below
Outputs:
- served: bfloat16 [2048, 8192], P(('groups', 'ranks'), 'tensor'), parts along dimension 0
- cache_store: bfloat16 [2048, 576], P(('groups', 'ranks')), parts along dimension 0
The draws below stay inside these ranges and needn't reach their ends.
There are 2 independent parts, one for each index of `groups`. The reference program is written for one: setup_inputs(seed, part) draws one part's arguments, and reference() takes and returns one part's arrays. A program takes and returns all parts, laid end to end along the dimension named above; an argument that names none is the same for every part. Nothing has to cross between parts.
Inputs may be any that keep to these rules, and one draw needn't show every extreme that they name: For each p, migrate[:, p] names every rank once, and the 8 pieces of one block go to every rank once. For each p, owners[:, p] names every rank once, and the 8 pieces of one block go to every rank once. `prompt_blocks`: the entries sum to 8.
All inputs are finite; a program needn't handle non-finite values.
Results may differ from the reference program's by a relative error of at most 0.012.
The reference program's roundings to bfloat16 on the way (of `cache_rows`, `probs`, `latent_out` and `head_out`) count: a program that leaves them out, or rounds other values in their place, can miss the bound.
Values may be sent and summed in bfloat16 or wider, within the bound.
A program may use at most 192 MiB of HBM per device.

```python
import math
import jax
import jax.numpy as jnp
import numpy as np
from jax import lax

D = 7168
LAT = 512
ROPE = 64
HEADS = 64
VDIM = 128
TOK_DEV = 128
KMAX = 4
NPROMPT = 4
PIECES = 8
PIECE_ROWS = 16
TOKENS = 1024
N_RANKS = 8


def spread_routes(key):
    order_key, shift_key = jax.random.split(key)
    ordering = jax.random.permutation(order_key, N_RANKS)
    offsets_drawn = jax.random.permutation(shift_key, N_RANKS)[:PIECES]
    rank_ids = jnp.arange(N_RANKS, dtype=jnp.int32)
    return jnp.take(ordering, (rank_ids[:, None] + offsets_drawn[None, :]) % N_RANKS).astype(jnp.int32)


def draw_queries(key, part):
    key = jax.random.fold_in(key, 11)
    first_key = jax.random.fold_in(key, 0)
    shape = (TOKENS, HEADS * (LAT + ROPE))
    values = jax.random.truncated_normal(first_key, -6.0, 6.0, shape, jnp.float32)
    return values.astype(jnp.bfloat16)


def draw_migrate(key, part):
    key = jax.random.fold_in(key, 21)
    return spread_routes(key)


def draw_owners(key, part):
    key = jax.random.fold_in(key, 31)
    return spread_routes(key)


def levels(own_key, extent, cuts, smallest, largest):
    gain = 1.0
    for axis_at, shards_of in cuts:
        heights = jax.random.uniform(jax.random.fold_in(jax.random.fold_in(own_key, 6), axis_at), (shards_of,), jnp.float32, smallest / len(cuts), largest / len(cuts))
        gain = gain * jnp.repeat(jnp.exp(heights), extent[axis_at] // shards_of).reshape((-1,) + (1,) * (len(extent) - 1 - axis_at))
    return gain


def profile(amount, total, limit, slope):
    weights = [(1 << 20) // math.isqrt(grade ** slope) + 1 for grade in range(2, amount + 1)]
    rest, given = total - limit - (amount - 1), [1] * (amount - 1)
    while rest > 0:
        movable = [i for i in range(amount - 1) if given[i] < limit]
        pool, remaining = sum([weights[i] for i in movable]), rest
        for i in movable:
            more = min(limit - given[i], max(1, remaining * weights[i] // pool), rest)
            given[i] = given[i] + more
            rest = rest - more
    return np.array([limit] + given)


def uneven_parts(own_key, amount, total, most, skew):
    if amount == 2:
        one = jax.random.randint(own_key, (), max(1, total - most), min(most, total - 1) + 1)
        return jnp.stack([one, total - one])
    sizes = jnp.asarray(profile(amount, total, most, skew), jnp.int32)
    couples = (amount - 1) // 2
    giver, taker = sizes[1:1 + 2 * couples:2], sizes[2:2 + 2 * couples:2]
    margin = jnp.minimum(giver - 1, most - taker)
    moved = jax.random.randint(jax.random.fold_in(own_key, 1), (couples,), 0, 1 << 20) % (margin + 1)
    sizes = sizes.at[1:1 + 2 * couples:2].set(giver - moved).at[2:2 + 2 * couples:2].set(taker + moved)
    return sizes[jax.random.permutation(jax.random.fold_in(own_key, 2), amount)]


def noise(stream_key, extent, deviation, bound, pieces=(), kind=jnp.bfloat16):
    array = deviation * jax.random.normal(stream_key, extent, jnp.float32)
    if pieces:
        array = array * levels(stream_key, extent, pieces, -0.22, 0.18)
    return jnp.clip(array, -bound, bound).astype(kind)


def setup_inputs(seed: int = 0, part: int = 0) -> dict:
    arg_keys = jax.random.split(jax.random.key(seed), 9)
    part_splits = jax.random.split(jax.random.fold_in(arg_keys[8], part), 9)
    return {
        "hidden": noise(part_splits[0], (TOKENS, D), 1.0, 6.0, ((0, 8), (1, 2))),
        "w_down": noise(arg_keys[1], (D, LAT + ROPE), D ** -0.5, 0.0625, ((0, 2),)),
        "latent_gain": jnp.clip(1.0 + 0.18 * jax.random.normal(arg_keys[2], (LAT,), jnp.float32), 0.099609375, 1.8984375).astype(jnp.bfloat16),
        "queries": draw_queries(jax.random.fold_in(jax.random.fold_in(arg_keys[8], part), 71), part),
        "w_up_value": noise(arg_keys[4], (HEADS, LAT, VDIM), LAT ** -0.5, 0.25, ((0, 2), (1, 8))),
        "prompt_blocks": uneven_parts(part_splits[5], NPROMPT, N_RANKS, KMAX, 1).astype(jnp.int32),
        "migrate": draw_migrate(jax.random.fold_in(jax.random.fold_in(arg_keys[8], part), 71), part),
        "owners": draw_owners(jax.random.fold_in(jax.random.fold_in(arg_keys[8], part), 71), part),
    }


def latent_rows(latent_raw, latent_gain):
    latent_part = latent_raw[:, :LAT]
    mean_square = lax.optimization_barrier(jnp.mean(latent_part * latent_part, axis=-1, keepdims=True))
    normed = latent_part * lax.rsqrt(mean_square + 1e-06) * latent_gain.astype(jnp.float32)
    return jnp.concatenate([normed, latent_raw[:, LAT:]], axis=-1).astype(jnp.bfloat16)

def block_starts(prompt_blocks):
    prompt_ends = jnp.cumsum(prompt_blocks).astype(jnp.int32)
    prompt_firsts = (prompt_ends - prompt_blocks).astype(jnp.int32)
    block_ids = jnp.arange(N_RANKS, dtype=jnp.int32)
    holder = lax.optimization_barrier(jnp.sum((block_ids[:, None] >= prompt_ends[None, :]).astype(jnp.int32), axis=1)).astype(jnp.int32)
    return jnp.take(prompt_firsts, holder).astype(jnp.int32)

def attend_block(block_index, queries, key_pad, w_up_value, starts):
    width = LAT + ROPE
    score_scale = 2.0 / math.sqrt(width)
    first_row = (block_index * TOK_DEV).astype(jnp.int32)
    query_rows = lax.dynamic_slice_in_dim(queries, first_row, TOK_DEV, 0).astype(jnp.float32)
    query_rows = query_rows.reshape(TOK_DEV, HEADS, width)
    window = lax.dynamic_slice_in_dim(key_pad, first_row, KMAX * TOK_DEV, 0).astype(jnp.float32)
    query_pos = first_row + jnp.arange(TOK_DEV, dtype=jnp.int32)
    key_pos = (block_index - (KMAX - 1)) * TOK_DEV + jnp.arange(KMAX * TOK_DEV, dtype=jnp.int32)
    first_key = jnp.take(starts, block_index) * TOK_DEV
    allowed = (key_pos[None, :] >= first_key) & (key_pos[None, :] <= query_pos[:, None])
    scores = jnp.einsum('thd,sd->hts', query_rows, window) * score_scale
    scores = jnp.where(allowed[None], scores, jnp.float32(-1e+30))
    highest = lax.optimization_barrier(jnp.max(scores, axis=-1, keepdims=True))
    expos = jnp.exp(scores - highest)
    probs = (expos / lax.optimization_barrier(jnp.sum(expos, axis=-1, keepdims=True))).astype(jnp.bfloat16)
    latent_out = jnp.einsum('hts,sl->thl', probs.astype(jnp.float32), window[:, :LAT]).astype(jnp.bfloat16)
    head_out = jnp.einsum('thl,hlv->thv', latent_out.astype(jnp.float32), w_up_value.astype(jnp.float32))
    return head_out.astype(jnp.bfloat16).reshape(TOK_DEV, HEADS * VDIM)

def place(blocks, routes):
    piece_ids = jnp.broadcast_to(jnp.arange(PIECES, dtype=jnp.int32)[None, :], routes.shape)
    return jnp.zeros_like(blocks).at[routes, piece_ids].set(blocks)

def reference(hidden, w_down, latent_gain, queries, w_up_value, prompt_blocks, migrate, owners):
    latent_raw = jnp.dot(hidden, w_down, preferred_element_type=jnp.float32)
    cache_rows = latent_rows(latent_raw, latent_gain)
    key_pad = jnp.concatenate([jnp.zeros(((KMAX - 1) * TOK_DEV, LAT + ROPE), jnp.bfloat16), cache_rows], axis=0)
    starts = block_starts(prompt_blocks)

    def one_block(block_index):
        return attend_block(block_index, queries, key_pad, w_up_value, starts)
    head_out = lax.map(one_block, jnp.arange(N_RANKS, dtype=jnp.int32))
    served = place(head_out.reshape(N_RANKS, PIECES, PIECE_ROWS, HEADS * VDIM), migrate)
    cache_store = place(cache_rows.reshape(N_RANKS, PIECES, PIECE_ROWS, LAT + ROPE), owners)
    return (served.reshape(TOKENS, HEADS * VDIM), cache_store.reshape(TOKENS, LAT + ROPE))
```

```python
import functools
import math

import jax
import jax.numpy as jnp
from jax import lax
from jax.experimental import pallas as pl
from jax.experimental.pallas import tpu as pltpu
from jax.sharding import PartitionSpec as P

LAT = 512
ROPE = 64


def passed_along(block, axis, distance):
    devices = range(lax.axis_size(axis))
    route = [(i - distance, i) for i in devices if i - distance in devices]
    return lax.ppermute(block, axis, route)


def normalize(latent_raw, latent_gain):
    latent_part = latent_raw[:, :LAT]
    mean_square = jnp.mean(latent_part * latent_part, axis=-1, keepdims=True)
    normed = latent_part * lax.rsqrt(mean_square + 1e-06) * latent_gain.astype(jnp.float32)
    return jnp.concatenate([normed, latent_raw[:, LAT:]], axis=-1).astype(jnp.bfloat16)


def block_starts(prompt_blocks, rank_count):
    prompt_ends = jnp.cumsum(prompt_blocks)
    prompt_firsts = prompt_ends - prompt_blocks
    block_ids = jnp.arange(rank_count, dtype=jnp.int32)
    holder = jnp.sum((block_ids[:, None] >= prompt_ends[None, :]).astype(jnp.int32), axis=1)
    return jnp.take(prompt_firsts, holder)


def send_buffer(values, routes, my_rank, rank_count):
    piece_count = routes.shape[1]
    pieces = values.reshape(piece_count, values.shape[0] // piece_count, values.shape[1])
    own_routes = jnp.take(routes, my_rank, axis=0)
    one_hot = (own_routes[None, :] == jnp.arange(rank_count, dtype=jnp.int32)[:, None]).astype(
        jnp.bfloat16
    )
    return jnp.einsum("dp,prc->drc", one_hot, pieces, preferred_element_type=jnp.float32).astype(
        jnp.bfloat16
    )


def pick_slots(received, routes, my_rank):
    selector = (jnp.transpose(routes) == my_rank).astype(jnp.bfloat16)
    placed = jnp.einsum("pr,rqc->pqc", selector, received, preferred_element_type=jnp.float32)
    return placed.astype(jnp.bfloat16).reshape(-1, received.shape[2])


def body(hidden, w_down, latent_gain, queries, w_up_value, prompt_blocks, migrate, owners):
    tok_rows = hidden.shape[0]
    width = LAT + ROPE
    partial_latent = jnp.dot(hidden, w_down, preferred_element_type=jnp.float32)
    summed = lax.psum(partial_latent, "tensor")
    cache_rows = normalize(summed, latent_gain)
    my_rank = lax.axis_index("ranks")
    rank_count = lax.axis_size("ranks")
    span = rank_count // 2
    window = cache_rows[None]
    for level in range(span.bit_length() - 1):
        incoming = passed_along(window, "ranks", 2**level)
        window = jnp.concatenate([incoming, window], axis=0)
    starts = block_starts(prompt_blocks, rank_count)
    first_block = jnp.take(starts, my_rank)
    first_key = first_block * tok_rows
    lowest = jnp.maximum(first_block - my_rank + span - 1, 0)
    query_pos = my_rank * tok_rows + jnp.arange(tok_rows, dtype=jnp.int32)
    local_heads = queries.shape[1] // width
    group_size = 16
    group_count = local_heads // group_size
    grouped = jnp.transpose(queries.reshape(tok_rows, group_count, group_size, width), (1, 0, 2, 3))
    score_scale = 2.0 / math.sqrt(width)

    def attend(query_group):
        empty = jnp.full((group_size, tok_rows, span * tok_rows), -1e30, jnp.float32)

        def fill(block, buffer):
            keys = lax.dynamic_index_in_dim(window, block, 0, keepdims=False)
            scores = (
                jnp.einsum("thd,sd->hts", query_group, keys, preferred_element_type=jnp.float32)
                * score_scale
            )
            key_pos = (my_rank - (span - 1) + block) * tok_rows + jnp.arange(
                tok_rows, dtype=jnp.int32
            )
            allowed = (key_pos[None, :] >= first_key) & (key_pos[None, :] <= query_pos[:, None])
            scores = jnp.where(allowed[None], scores, jnp.float32(-1e30))
            return lax.dynamic_update_slice_in_dim(buffer, scores, block * tok_rows, 2)

        scores = lax.fori_loop(lowest, span, fill, empty)
        highest = jnp.max(scores, axis=-1, keepdims=True)
        expos = jnp.exp(scores - highest)
        probs = (expos / jnp.sum(expos, axis=-1, keepdims=True)).astype(jnp.bfloat16)

        def collect(block, running):
            weights = lax.dynamic_slice_in_dim(probs, block * tok_rows, tok_rows, 2)
            keys = lax.dynamic_index_in_dim(window, block, 0, keepdims=False)[:, :LAT]
            return running + jnp.einsum(
                "hts,sl->thl", weights, keys, preferred_element_type=jnp.float32
            )

        start_out = jnp.zeros((tok_rows, group_size, LAT), jnp.float32)
        return lax.fori_loop(lowest, span, collect, start_out).astype(jnp.bfloat16)

    grouped_out = lax.map(attend, grouped)
    latent_out = jnp.transpose(grouped_out, (1, 0, 2, 3)).reshape(tok_rows, local_heads, LAT)
    summed_values = jnp.einsum(
        "thl,hlv->thv",
        latent_out,
        lax.all_gather(w_up_value, "ranks", axis=1, tiled=True),
        preferred_element_type=jnp.float32,
    )
    head_out = summed_values.astype(jnp.bfloat16).reshape(
        tok_rows, local_heads * w_up_value.shape[2]
    )
    outgoing = send_buffer(head_out, migrate, my_rank, rank_count)
    arrived = lax.all_to_all(outgoing, "ranks", split_axis=0, concat_axis=0, tiled=True)
    served = pick_slots(arrived, migrate, my_rank)
    cache_out = send_buffer(cache_rows, owners, my_rank, rank_count)
    cache_in = lax.all_to_all(cache_out, "ranks", split_axis=0, concat_axis=0, tiled=True)
    cache_store = pick_slots(cache_in, owners, my_rank)
    return (served, cache_store)


PIECE = 16
WIDE = LAT + 2 * ROPE
BLOCKS = 4
GROUPS = 4
MESH = pl.DeviceIdType.MESH


def remote(src, dst, send_sem, recv_sem, where):
    return pltpu.make_async_remote_copy(
        src_ref=src,
        dst_ref=dst,
        send_sem=send_sem,
        recv_sem=recv_sem,
        device_id=where,
        device_id_type=MESH,
    )


def by_piece(index, values):
    out = jnp.zeros_like(index)
    for p, value in enumerate(values):
        out = jnp.where((index // PIECE) == p, value, out)
    return out


def send_matrix(routes, me, n):
    rows = lax.broadcasted_iota(jnp.int32, (n * PIECE, n * PIECE), 0)
    cols = lax.broadcasted_iota(jnp.int32, (n * PIECE, n * PIECE), 1)
    target = by_piece(cols, [routes[me, p] for p in range(n)])
    hit = ((rows // PIECE) == target) & ((rows % PIECE) == (cols % PIECE))
    return jnp.where(hit, 1.0, 0.0).astype(jnp.bfloat16)


def take_matrix(routes, me, n):
    rows = lax.broadcasted_iota(jnp.int32, (n * PIECE, n * PIECE), 0)
    cols = lax.broadcasted_iota(jnp.int32, (n * PIECE, n * PIECE), 1)
    origins = []
    for p in range(n):
        origin = jnp.int32(0)
        for r in range(n):
            origin = origin + jnp.where(routes[r, p] == me, r, 0)
        origins.append(origin)
    source = by_piece(rows, origins)
    hit = ((cols // PIECE) == source) & ((rows % PIECE) == (cols % PIECE))
    return jnp.where(hit, 1.0, 0.0).astype(jnp.bfloat16)


def kernel(
    n, hidden, w_down, gain, queries, w_up, prompt_blocks, migrate, owners,
    served, store,
    hid, wd, qbuf, wall, part, part_in, key0, key1, latent, bias, out_mat, in_mat,
    send, recv, csend, crecv,
    hid_sem, wd_sem, q_sem, own_sem, part_sem, key_send, key_recv,
    y_send, up_send, down_send, x_send, w_recv, send_sem, recv_sem, c_send, c_recv,
):
    me = lax.axis_index("ranks")
    x = lax.axis_index("groups")
    core = lax.axis_index("tensor")
    z, y = me // 2, me % 2
    levels = n // 2
    tok = hid.shape[0]
    heads = w_up.shape[0]
    half = heads // 2
    pairs = heads // 2
    twin = 2 * z + (1 - y)
    other_x = {"groups": 1 - x}

    chunks = wd_sem.shape[0]
    rows = wd.shape[0] // chunks
    hid_copy = pltpu.make_async_copy(hidden, hid, hid_sem)
    hid_copy.start()
    wd_copies = []
    for c in range(chunks):
        cut = pl.ds(c * rows, rows)
        wd_copies.append(pltpu.make_async_copy(w_down.at[cut], wd.at[cut], wd_sem.at[c]))
        wd_copies[-1].start()

    barrier = pltpu.get_barrier_semaphore()
    for k in range(1, n):
        pl.semaphore_signal(barrier, 1, device_id={"ranks": (me + k) % n}, device_id_type=MESH)
    pl.semaphore_signal(barrier, 1, device_id={"tensor": 1 - core}, device_id_type=MESH)
    pl.semaphore_signal(barrier, 1, device_id=other_x, device_id_type=MESH)
    pl.semaphore_wait(barrier, n + 1)

    def hcut(h):
        return pl.ds(h * half, half)

    def slot(r, h):
        return wall.at[r, hcut(h)]

    def hop(sems, src, r, h, where):
        return remote(src, slot(r, h), sems.at[r, h], w_recv.at[r, h], where)

    y_first = hop(y_send, w_up.at[hcut(x)], me, x, {"ranks": twin})
    y_last = hop(y_send, w_up.at[hcut(1 - x)], me, 1 - x, {"ranks": twin})
    own_copy = pltpu.make_async_copy(w_up, wall.at[me], own_sem)

    def up_hop(r, src):
        return hop(up_send, src, r, x, {"ranks": jnp.minimum(me + 2, n - 2 + y)})

    def down_hop(r, src):
        return hop(down_send, src, r, x, {"ranks": jnp.maximum(me - 2, y)})

    def x_hop(r):
        return hop(x_send, slot(r, x), r, x, other_x)

    def arrived(r, h):
        remote(slot(r, h), slot(r, h), x_send.at[r, h], w_recv.at[r, h], other_x).wait_recv()

    y_first.start()

    @pl.when(z < levels - 1)
    def _():
        up_hop(me, w_up.at[hcut(x)]).start()

    @pl.when(z > 0)
    def _():
        down_hop(me, w_up.at[hcut(x)]).start()

    q_copies = []
    for parity in range(2):
        for i in range(pairs):
            q_copies.append(
                pltpu.make_async_copy(
                    queries.at[:, pl.ds(i * 2 * (LAT + ROPE) + parity * LAT, WIDE)],
                    qbuf.at[parity, i],
                    q_sem.at[parity, i],
                )
            )
            q_copies[-1].start()
    own_copy.start()
    y_last.start()

    hid_copy.wait()
    for c in range(chunks):
        wd_copies[c].wait()
        term = jnp.dot(
            hid[:, c * rows : (c + 1) * rows],
            wd[c * rows : (c + 1) * rows, :],
            preferred_element_type=jnp.float32,
        )
        part[...] = term if c == 0 else part[...] + term
    part_copy = remote(part, part_in, part_sem.at[0], part_sem.at[1], {"tensor": 1 - core})
    part_copy.start()

    out_mat[0] = send_matrix(migrate, me, n)
    out_mat[1] = send_matrix(owners, me, n)
    in_mat[0] = take_matrix(migrate, me, n)
    in_mat[1] = take_matrix(owners, me, n)
    first = jnp.int32(0)
    end = jnp.int32(0)
    for i in range(prompt_blocks.shape[0]):
        end = end + prompt_blocks[i]
        first = jnp.where(me >= end, end, first)
    query_pos = me * tok + lax.broadcasted_iota(jnp.int32, (tok, BLOCKS * tok), 0)
    key_pos = (me - (BLOCKS - 1)) * tok + lax.broadcasted_iota(jnp.int32, (tok, BLOCKS * tok), 1)
    allowed = (key_pos >= first * tok) & (key_pos <= query_pos)
    bias[...] = jnp.where(allowed, 0.0, -1e30)

    part_copy.wait()
    raw = part[...] + part_in[...]
    lead = raw[:, :LAT]
    mean_square = jnp.mean(lead * lead, axis=-1, keepdims=True)
    normed = lead * lax.rsqrt(mean_square + 1e-06) * gain[...].astype(jnp.float32)
    rope = raw[:, LAT:]
    blank = jnp.zeros((tok, ROPE), jnp.float32)
    key0[BLOCKS - 1] = jnp.concatenate([normed, rope, blank], axis=-1).astype(jnp.bfloat16)

    def key_copy(d, r):
        return remote(
            key0.at[BLOCKS - 1], key0.at[BLOCKS - 1 - d], key_send.at[d], key_recv.at[d], {"ranks": r}
        )

    for d in range(1, BLOCKS):
        @pl.when(me + d < n)
        def _():
            key_copy(d, (me + d) % n).start()

    arrived(twin, x)

    @pl.when(z < levels - 1)
    def _():
        up_hop(twin, slot(twin, x)).start()

    @pl.when(z > 0)
    def _():
        down_hop(twin, slot(twin, x)).start()

    csend[...] = (
        jnp.dot(out_mat[1], key0[BLOCKS - 1], preferred_element_type=jnp.float32)
        .astype(jnp.bfloat16)
        .reshape(n, PIECE, WIDE)
    )
    crecv[me] = csend[me]

    def c_copy(k):
        to = (me + k) % n
        return remote(csend.at[to], crecv.at[me], c_send.at[to], c_recv.at[me], {"ranks": to})

    for k in range(1, n):
        c_copy(k).start()

    for d in range(1, BLOCKS):
        @pl.when(me >= d)
        def _():
            key_copy(d, (me + d) % n).wait_recv()

        @pl.when(me < d)
        def _():
            key0[BLOCKS - 1 - d] = jnp.zeros((tok, WIDE), jnp.bfloat16)

    for b in range(BLOCKS):
        key1[b] = jnp.concatenate(
            [jnp.zeros((tok, ROPE), jnp.bfloat16), key0[b][:, : LAT + ROPE]], axis=-1
        )

    def relay(d, same):
        def row(level):
            return 2 * level + (y if same else 1 - y)

        @pl.when(z >= d)
        def _():
            r = row(jnp.maximum(z - d, 0))
            arrived(r, x)
            if d < levels - 1:
                @pl.when(z < levels - 1)
                def _():
                    up_hop(r, slot(r, x)).start()

            x_hop(r).start()

        @pl.when(z + d < levels)
        def _():
            r = row(jnp.minimum(z + d, levels - 1))
            arrived(r, x)
            if d < levels - 1:
                @pl.when(z > 0)
                def _():
                    down_hop(r, slot(r, x)).start()

            x_hop(r).start()

    factor = 2.0 / math.sqrt(LAT + ROPE) * math.log2(math.e)
    step = 4

    def attend(parity, keys, g):
        at = pl.ds(g * step, step)
        q = qbuf[parity, at].reshape(step * tok, WIDE)
        s = lax.dot_general(
            q,
            keys[...].reshape(BLOCKS * tok, WIDE),
            (((1,), (1,)), ((), ())),
            preferred_element_type=jnp.float32,
        )
        s = s.reshape(step, tok, BLOCKS * tok) + bias[...][None]
        top = jnp.max(s, axis=-1, keepdims=True)
        e = jnp.exp2((s - top) * factor)
        p = (e * (1.0 / jnp.sum(e, axis=-1, keepdims=True))).astype(jnp.bfloat16)
        out = jnp.dot(
            p.reshape(step * tok, BLOCKS * tok),
            key0[:, :, :LAT].reshape(BLOCKS * tok, LAT),
            preferred_element_type=jnp.float32,
        )
        latent[parity, at] = out.astype(jnp.bfloat16).reshape(step, tok, LAT)

    events = [(d, same) for d in range(1, levels) for same in (True, False)]
    plan = [events[:1], events[1:2], events[2:3], events[3:4], events[4:]]
    for copy in q_copies:
        copy.wait()
    spots = iter(plan)
    for parity, keys in ((0, key0), (1, key1)):
        for lower in (0, 2):
            for event in next(spots):
                relay(*event)

            def some(g, carry, parity=parity, keys=keys):
                attend(parity, keys, g)
                return carry

            lax.fori_loop(lower, lower + 2, some, 0)
    for event in next(spots):
        relay(*event)

    group = heads // GROUPS
    wide = group * w_up.shape[2]
    vdim = w_up.shape[2]

    def gcols(g):
        return pl.ds(pl.multiple_of(g * wide, wide), wide)

    def piece_copy(g, k):
        to = (me + k) % n
        return remote(
            send.at[to, :, gcols(g)],
            recv.at[me, :, gcols(g)],
            send_sem.at[g, to],
            recv_sem.at[g, me],
            {"ranks": to},
        )

    def project(g):
        def one(i, carry):
            for parity in range(2):
                h = g * group + 2 * i + parity
                w = wall[:, h].reshape(LAT, vdim)
                out = jnp.dot(
                    latent[parity, g * (group // 2) + i], w, preferred_element_type=jnp.float32
                ).astype(jnp.bfloat16)
                moved = jnp.dot(out_mat[0], out, preferred_element_type=jnp.float32)
                cols = pl.ds(pl.multiple_of(h * vdim, vdim), vdim)
                send[:, :, cols] = moved.astype(jnp.bfloat16).reshape(n, PIECE, vdim)
            return carry

        lax.fori_loop(0, group // 2, one, 0)
        for k in range(1, n):
            piece_copy(g, k).start()
        recv[me, :, gcols(g)] = send[me, :, gcols(g)]

    own_copy.wait()
    for i in range(GROUPS // 2):
        project(x * (GROUPS // 2) + i)
    arrived(twin, 1 - x)
    for d in range(1, levels):
        for same in (True, False):
            def row(level):
                return 2 * level + (y if same else 1 - y)

            @pl.when(z >= d)
            def _():
                arrived(row(jnp.maximum(z - d, 0)), 1 - x)

            @pl.when(z + d < levels)
            def _():
                arrived(row(jnp.minimum(z + d, levels - 1)), 1 - x)

    for i in range(GROUPS // 2):
        project((1 - x) * (GROUPS // 2) + i)

    for k in range(1, n):
        r = (me + k) % n
        remote(csend.at[r], crecv.at[r], c_send.at[r], c_recv.at[r], {"ranks": r}).wait_recv()
    kept = jnp.dot(
        in_mat[1], crecv[...].reshape(n * PIECE, WIDE), preferred_element_type=jnp.float32
    )
    store[...] = kept[:, : LAT + ROPE].astype(jnp.bfloat16)
    for i in range(GROUPS):
        g = (x * (GROUPS // 2) + i) % GROUPS
        for k in range(1, n):
            r = (me + k) % n
            remote(
                send.at[r, :, gcols(g)],
                recv.at[r, :, gcols(g)],
                send_sem.at[g, r],
                recv_sem.at[g, r],
                {"ranks": r},
            ).wait_recv()
        served[:, gcols(g)] = jnp.dot(
            in_mat[0],
            recv[:, :, gcols(g)].reshape(n * PIECE, wide),
            preferred_element_type=jnp.float32,
        ).astype(jnp.bfloat16)

    y_first.wait_send()
    y_last.wait_send()
    for d in range(1, BLOCKS):
        @pl.when(me + d < n)
        def _():
            key_copy(d, (me + d) % n).wait_send()

    for k in range(1, n):
        c_copy(k).wait_send()
        for g in range(GROUPS):
            piece_copy(g, k).wait_send()
    for level_at in range(levels):
        for same in (True, False):
            r = 2 * level_at + (y if same else 1 - y)

            @pl.when((z >= level_at) & (z < levels - 1))
            def _():
                up_hop(r, slot(r, x)).wait_send()

            @pl.when((z <= level_at) & (z > 0))
            def _():
                down_hop(r, slot(r, x)).wait_send()

            @pl.when(z != level_at)
            def _():
                x_hop(r).wait_send()


def fused(hidden, w_down, latent_gain, queries, w_up_value, prompt_blocks, migrate, owners):
    n = lax.axis_size("ranks")
    tok, depth = hidden.shape
    heads, _, vdim = w_up_value.shape
    any_space = pl.BlockSpec(memory_space=pl.ANY)
    vmem = pl.BlockSpec(memory_space=pltpu.VMEM)
    smem = pl.BlockSpec(memory_space=pltpu.SMEM)
    bf16 = jnp.bfloat16
    dma = pltpu.SemaphoreType.DMA
    return pl.pallas_call(
        functools.partial(kernel, n),
        out_shape=(
            jax.ShapeDtypeStruct((tok, heads * vdim), bf16),
            jax.ShapeDtypeStruct((tok, LAT + ROPE), bf16),
        ),
        in_specs=[any_space, any_space, vmem, any_space, any_space, smem, smem, smem],
        out_specs=(vmem, vmem),
        scratch_shapes=[
            pltpu.VMEM((tok, depth), bf16),
            pltpu.VMEM((depth, LAT + ROPE), bf16),
            pltpu.VMEM((2, heads // 2, tok, WIDE), bf16),
            pltpu.VMEM((n, heads, w_up_value.shape[1], vdim), bf16),
            pltpu.VMEM((tok, LAT + ROPE), jnp.float32),
            pltpu.VMEM((tok, LAT + ROPE), jnp.float32),
            pltpu.VMEM((BLOCKS, tok, WIDE), bf16),
            pltpu.VMEM((BLOCKS, tok, WIDE), bf16),
            pltpu.VMEM((2, heads // 2, tok, LAT), bf16),
            pltpu.VMEM((tok, BLOCKS * tok), jnp.float32),
            pltpu.VMEM((2, tok, tok), bf16),
            pltpu.VMEM((2, tok, tok), bf16),
            pltpu.VMEM((n, PIECE, heads * vdim), bf16),
            pltpu.VMEM((n, PIECE, heads * vdim), bf16),
            pltpu.VMEM((n, PIECE, WIDE), bf16),
            pltpu.VMEM((n, PIECE, WIDE), bf16),
            dma(()),
            dma((4,)),
            dma((2, heads // 2)),
            dma(()),
            dma((2,)),
            dma((BLOCKS,)),
            dma((BLOCKS,)),
            dma((n, 2)),
            dma((n, 2)),
            dma((n, 2)),
            dma((n, 2)),
            dma((n, 2)),
            dma((GROUPS, n)),
            dma((GROUPS, n)),
            dma((n,)),
            dma((n,)),
        ],
        compiler_params=pltpu.CompilerParams(
            collective_id=0, has_side_effects=True, vmem_limit_bytes=52 * 1024 * 1024
        ),
    )(
        hidden, w_down, latent_gain.reshape(1, LAT), queries, w_up_value,
        prompt_blocks, migrate, owners,
    )


def solution(mesh):
    sizes = dict(mesh.shape)
    small = sizes["ranks"] == 8 and sizes["groups"] == 2 and sizes["tensor"] == 2
    placed = (
        P(("groups", "ranks"), "tensor"),
        P("tensor", None),
        P(),
        P(("groups", "ranks"), "tensor"),
        P("tensor", "ranks", None),
        P("groups"),
        P("groups", None),
        P("groups", None),
    )
    return jax.shard_map(
        fused if small else body,
        mesh=mesh,
        in_specs=placed,
        out_specs=(P(("groups", "ranks"), "tensor"), P(("groups", "ranks"), None)),
        check_vma=False,
    )
```

```python
import functools
import math

import jax
import jax.numpy as jnp
from jax import lax
from jax.experimental import pallas as pl
from jax.experimental.pallas import tpu as pltpu
from jax.sharding import PartitionSpec as P

LAT = 512
ROPE = 64


def passed_along(block, axis, distance):
    devices = range(lax.axis_size(axis))
    route = [(i - distance, i) for i in devices if i - distance in devices]
    return lax.ppermute(block, axis, route)


def normalize(latent_raw, latent_gain):
    latent_part = latent_raw[:, :LAT]
    mean_square = jnp.mean(latent_part * latent_part, axis=-1, keepdims=True)
    normed = latent_part * lax.rsqrt(mean_square + 1e-06) * latent_gain.astype(jnp.float32)
    return jnp.concatenate([normed, latent_raw[:, LAT:]], axis=-1).astype(jnp.bfloat16)


def block_starts(prompt_blocks, rank_count):
    prompt_ends = jnp.cumsum(prompt_blocks)
    prompt_firsts = prompt_ends - prompt_blocks
    block_ids = jnp.arange(rank_count, dtype=jnp.int32)
    holder = jnp.sum((block_ids[:, None] >= prompt_ends[None, :]).astype(jnp.int32), axis=1)
    return jnp.take(prompt_firsts, holder)


def send_buffer(values, routes, my_rank, rank_count):
    piece_count = routes.shape[1]
    pieces = values.reshape(piece_count, values.shape[0] // piece_count, values.shape[1])
    own_routes = jnp.take(routes, my_rank, axis=0)
    one_hot = (own_routes[None, :] == jnp.arange(rank_count, dtype=jnp.int32)[:, None]).astype(
        jnp.bfloat16
    )
    return jnp.einsum("dp,prc->drc", one_hot, pieces, preferred_element_type=jnp.float32).astype(
        jnp.bfloat16
    )


def pick_slots(received, routes, my_rank):
    selector = (jnp.transpose(routes) == my_rank).astype(jnp.bfloat16)
    placed = jnp.einsum("pr,rqc->pqc", selector, received, preferred_element_type=jnp.float32)
    return placed.astype(jnp.bfloat16).reshape(-1, received.shape[2])


def body(hidden, w_down, latent_gain, queries, w_up_value, prompt_blocks, migrate, owners):
    tok_rows = hidden.shape[0]
    width = LAT + ROPE
    partial_latent = jnp.dot(hidden, w_down, preferred_element_type=jnp.float32)
    summed = lax.psum(partial_latent, "tensor")
    cache_rows = normalize(summed, latent_gain)
    my_rank = lax.axis_index("ranks")
    rank_count = lax.axis_size("ranks")
    span = rank_count // 2
    window = cache_rows[None]
    for level in range(span.bit_length() - 1):
        incoming = passed_along(window, "ranks", 2**level)
        window = jnp.concatenate([incoming, window], axis=0)
    starts = block_starts(prompt_blocks, rank_count)
    first_block = jnp.take(starts, my_rank)
    first_key = first_block * tok_rows
    lowest = jnp.maximum(first_block - my_rank + span - 1, 0)
    query_pos = my_rank * tok_rows + jnp.arange(tok_rows, dtype=jnp.int32)
    local_heads = queries.shape[1] // width
    group_size = 16
    group_count = local_heads // group_size
    grouped = jnp.transpose(queries.reshape(tok_rows, group_count, group_size, width), (1, 0, 2, 3))
    score_scale = 2.0 / math.sqrt(width)

    def attend(query_group):
        empty = jnp.full((group_size, tok_rows, span * tok_rows), -1e30, jnp.float32)

        def fill(block, buffer):
            keys = lax.dynamic_index_in_dim(window, block, 0, keepdims=False)
            scores = (
                jnp.einsum("thd,sd->hts", query_group, keys, preferred_element_type=jnp.float32)
                * score_scale
            )
            key_pos = (my_rank - (span - 1) + block) * tok_rows + jnp.arange(
                tok_rows, dtype=jnp.int32
            )
            allowed = (key_pos[None, :] >= first_key) & (key_pos[None, :] <= query_pos[:, None])
            scores = jnp.where(allowed[None], scores, jnp.float32(-1e30))
            return lax.dynamic_update_slice_in_dim(buffer, scores, block * tok_rows, 2)

        scores = lax.fori_loop(lowest, span, fill, empty)
        highest = jnp.max(scores, axis=-1, keepdims=True)
        expos = jnp.exp(scores - highest)
        probs = (expos / jnp.sum(expos, axis=-1, keepdims=True)).astype(jnp.bfloat16)

        def collect(block, running):
            weights = lax.dynamic_slice_in_dim(probs, block * tok_rows, tok_rows, 2)
            keys = lax.dynamic_index_in_dim(window, block, 0, keepdims=False)[:, :LAT]
            return running + jnp.einsum(
                "hts,sl->thl", weights, keys, preferred_element_type=jnp.float32
            )

        start_out = jnp.zeros((tok_rows, group_size, LAT), jnp.float32)
        return lax.fori_loop(lowest, span, collect, start_out).astype(jnp.bfloat16)

    grouped_out = lax.map(attend, grouped)
    latent_out = jnp.transpose(grouped_out, (1, 0, 2, 3)).reshape(tok_rows, local_heads, LAT)
    summed_values = jnp.einsum(
        "thl,hlv->thv",
        latent_out,
        lax.all_gather(w_up_value, "ranks", axis=1, tiled=True),
        preferred_element_type=jnp.float32,
    )
    head_out = summed_values.astype(jnp.bfloat16).reshape(
        tok_rows, local_heads * w_up_value.shape[2]
    )
    outgoing = send_buffer(head_out, migrate, my_rank, rank_count)
    arrived = lax.all_to_all(outgoing, "ranks", split_axis=0, concat_axis=0, tiled=True)
    served = pick_slots(arrived, migrate, my_rank)
    cache_out = send_buffer(cache_rows, owners, my_rank, rank_count)
    cache_in = lax.all_to_all(cache_out, "ranks", split_axis=0, concat_axis=0, tiled=True)
    cache_store = pick_slots(cache_in, owners, my_rank)
    return (served, cache_store)


PIECE = 16
WIDE = LAT + 2 * ROPE
BLOCKS = 4
GROUPS = 4
MESH = pl.DeviceIdType.MESH


def remote(src, dst, send_sem, recv_sem, where):
    return pltpu.make_async_remote_copy(
        src_ref=src,
        dst_ref=dst,
        send_sem=send_sem,
        recv_sem=recv_sem,
        device_id=where,
        device_id_type=MESH,
    )


def by_piece(index, values):
    out = jnp.zeros_like(index)
    for p, value in enumerate(values):
        out = jnp.where((index // PIECE) == p, value, out)
    return out


def send_matrix(routes, me, n):
    rows = lax.broadcasted_iota(jnp.int32, (n * PIECE, n * PIECE), 0)
    cols = lax.broadcasted_iota(jnp.int32, (n * PIECE, n * PIECE), 1)
    target = by_piece(cols, [routes[me, p] for p in range(n)])
    hit = ((rows // PIECE) == target) & ((rows % PIECE) == (cols % PIECE))
    return jnp.where(hit, 1.0, 0.0).astype(jnp.bfloat16)


def take_matrix(routes, me, n):
    rows = lax.broadcasted_iota(jnp.int32, (n * PIECE, n * PIECE), 0)
    cols = lax.broadcasted_iota(jnp.int32, (n * PIECE, n * PIECE), 1)
    origins = []
    for p in range(n):
        origin = jnp.int32(0)
        for r in range(n):
            origin = origin + jnp.where(routes[r, p] == me, r, 0)
        origins.append(origin)
    source = by_piece(rows, origins)
    hit = ((cols // PIECE) == source) & ((rows % PIECE) == (cols % PIECE))
    return jnp.where(hit, 1.0, 0.0).astype(jnp.bfloat16)


def kernel(
    n, hidden, w_down, gain_in, queries, w_up, blocks_in, migrate_in, owners_in,
    served, store,
    hid, wd, qbuf, wall, part, part_in, key0, key1, latent, bias, out_mat, in_mat,
    send, recv, csend, crecv,
    gain, prompt_blocks, migrate, owners, small_sem,
    hid_sem, wd_sem, q_sem, own_sem, part_sem, key_send, key_recv,
    share_send, share_recv, c_share_send, c_share_recv,
    y_send, up_send, down_send, x_send, w_recv, send_sem, recv_sem, c_send, c_recv,
):
    me = lax.axis_index("ranks")
    x = lax.axis_index("groups")
    core = lax.axis_index("tensor")
    z, y = me // 2, me % 2
    levels = n // 2
    tok = hid.shape[0]
    heads = w_up.shape[0]
    half = heads // 2
    pairs = heads // 2
    twin = 2 * z + (1 - y)
    other_x = {"groups": 1 - x}

    chunks = wd_sem.shape[0]
    rows = wd.shape[1] // chunks
    hid_copy = pltpu.make_async_copy(hidden, hid, hid_sem)
    hid_copy.start()
    wd_copies = []
    for c in range(chunks):
        cut = pl.ds(c * rows, rows)
        wd_copies.append(
            pltpu.make_async_copy(w_down.at[:, cut], wd.at[:, cut], wd_sem.at[c])
        )
        wd_copies[-1].start()

    small = [
        pltpu.make_async_copy(src, dst, small_sem.at[i])
        for i, (src, dst) in enumerate(
            ((gain_in, gain), (blocks_in, prompt_blocks), (migrate_in, migrate), (owners_in, owners))
        )
    ]
    for copy in small:
        copy.start()

    barrier = pltpu.get_barrier_semaphore()
    for k in range(1, n):
        pl.semaphore_signal(barrier, 1, device_id={"ranks": (me + k) % n}, device_id_type=MESH)
    pl.semaphore_signal(barrier, 1, device_id={"tensor": 1 - core}, device_id_type=MESH)
    pl.semaphore_signal(barrier, 1, device_id=other_x, device_id_type=MESH)
    pl.semaphore_wait(barrier, n + 1)

    quarter = half // 2

    def near(r, h, other):
        return wall.at[r, pl.ds(h * half, quarter if other else half)]

    def far(r, h):
        return wall.at[r, pl.ds(h * half + quarter, quarter)]

    def own(h, other):
        return w_up.at[pl.ds(h * half, quarter if other else half)]

    def y_own(h):
        return remote(own(h, False), near(me, h, False), y_send.at[me, h], w_recv.at[me, h, 0], {"ranks": twin})

    def y_far(r, h):
        return remote(far(r, h), far(r, h), y_send.at[r, h], w_recv.at[r, h, 1], {"ranks": twin})

    def up_hop(r, src, other):
        to = {"ranks": jnp.minimum(me + 2, n - 2 + y)}
        return remote(src, near(r, x, other), up_send.at[r], w_recv.at[r, x, 0], to)

    def down_hop(r, src, other):
        to = {"ranks": jnp.maximum(me - 2, y)}
        return remote(src, near(r, x, other), down_send.at[r], w_recv.at[r, x, 0], to)

    def x_hop(r, other):
        return remote(near(r, x, other), near(r, x, other), x_send.at[r], w_recv.at[r, x, 0], other_x)

    def arrived(r, h, other):
        remote(near(r, h, other), near(r, h, other), x_send.at[r], w_recv.at[r, h, 0], other_x).wait_recv()

    own_copy = pltpu.make_async_copy(w_up, wall.at[me], own_sem)

    def at_levels(d, other, act):
        for sign, within in ((-1, z >= d), (1, z + d < levels)):
            @pl.when(within)
            def _():
                level = jnp.clip(z + sign * d, 0, levels - 1)
                act(2 * level + (1 - y if other else y), sign)

    def relay(d, same):
        other = not same

        def act(r, sign):
            arrived(r, x, other)
            if d < levels - 1:
                if sign < 0:
                    @pl.when(z < levels - 1)
                    def _():
                        up_hop(r, near(r, x, other), other).start()
                else:
                    @pl.when(z > 0)
                    def _():
                        down_hop(r, near(r, x, other), other).start()

            x_hop(r, other).start()
            if same:
                y_far(r, x).start()

        at_levels(d, other, act)

    def relay_x(d):
        def act(r, sign):
            arrived(r, 1 - x, False)
            y_far(r, 1 - x).start()

        at_levels(d, False, act)

    def gathered(h):
        def act(r, sign):
            if h is None:
                arrived(r, 1 - x, True)
                y_far(r, 1 - x).wait_recv()
            else:
                y_far(r, x).wait_recv()

        for d in range(1, levels):
            at_levels(d, True, act)

    y_own(x).start()

    @pl.when(z < levels - 1)
    def _():
        up_hop(me, own(x, False), False).start()

    @pl.when(z > 0)
    def _():
        down_hop(me, own(x, False), False).start()

    q_copies = []
    for parity in range(2):
        for i in range(pairs):
            q_copies.append(
                pltpu.make_async_copy(
                    queries.at[:, pl.ds(i * 2 * (LAT + ROPE) + parity * LAT, WIDE)],
                    qbuf.at[parity, i],
                    q_sem.at[parity, i],
                )
            )
            q_copies[-1].start()
    own_copy.start()
    y_own(1 - x).start()

    hid_copy.wait()
    for c in range(chunks):
        wd_copies[c].wait()
        term = lax.dot_general(
            hid[:, c * rows : (c + 1) * rows],
            wd[:, c * rows : (c + 1) * rows],
            (((1,), (1,)), ((), ())),
            preferred_element_type=jnp.float32,
        )
        part[...] = term if c == 0 else part[...] + term
    part_copy = remote(part, part_in, part_sem.at[0], part_sem.at[1], {"tensor": 1 - core})
    part_copy.start()

    arrived(twin, x, False)

    @pl.when(z < levels - 1)
    def _():
        up_hop(twin, near(twin, x, True), True).start()

    @pl.when(z > 0)
    def _():
        down_hop(twin, near(twin, x, True), True).start()

    relay(1, True)
    for copy in small:
        copy.wait()
    out_mat[0] = send_matrix(migrate, me, n)
    out_mat[1] = send_matrix(owners, me, n)
    in_mat[0] = take_matrix(migrate, me, n)
    in_mat[1] = take_matrix(owners, me, n)
    first = jnp.int32(0)
    end = jnp.int32(0)
    for i in range(prompt_blocks.shape[0]):
        end = end + prompt_blocks[i]
        first = jnp.where(me >= end, end, first)
    query_pos = me * tok + lax.broadcasted_iota(jnp.int32, (tok, BLOCKS * tok), 0)
    key_pos = (me - (BLOCKS - 1)) * tok + lax.broadcasted_iota(jnp.int32, (tok, BLOCKS * tok), 1)
    allowed = (key_pos >= first * tok) & (key_pos <= query_pos)
    bias[...] = jnp.where(allowed, 0.0, -1e30)

    part_copy.wait()
    raw = part[...] + part_in[...]
    lead = raw[:, :LAT]
    mean_square = jnp.mean(lead * lead, axis=-1, keepdims=True)
    normed = lead * lax.rsqrt(mean_square + 1e-06) * gain[...].astype(jnp.float32).reshape(1, LAT)
    rope = raw[:, LAT:]
    blank = jnp.zeros((tok, ROPE), jnp.float32)
    key0[BLOCKS - 1] = jnp.concatenate([normed, rope, blank], axis=-1).astype(jnp.bfloat16)

    my_rows = pl.ds(core * (tok // 2), tok // 2)
    its_rows = pl.ds((1 - core) * (tok // 2), tok // 2)

    def key_copy(d, r):
        return remote(
            key0.at[BLOCKS - 1, my_rows],
            key0.at[BLOCKS - 1 - d, my_rows],
            key_send.at[d],
            key_recv.at[d],
            {"ranks": r},
        )

    def key_share(d, part_rows):
        block = key0.at[BLOCKS - 1 - d, part_rows]
        return remote(block, block, share_send.at[d], share_recv.at[d], {"tensor": 1 - core})

    for d in range(1, BLOCKS):
        @pl.when(me + d < n)
        def _():
            key_copy(d, (me + d) % n).start()

    relay(1, False)
    csend[...] = (
        jnp.dot(out_mat[1], key0[BLOCKS - 1], preferred_element_type=jnp.float32)
        .astype(jnp.bfloat16)
        .reshape(n, PIECE, WIDE)
    )
    crecv[me] = csend[me]

    def c_copy(k):
        to = (me + k) % n
        return remote(csend.at[to], crecv.at[me], c_send.at[to], c_recv.at[me], {"ranks": to})

    @pl.when(y == core)
    def _():
        for k in range(1, n):
            c_copy(k).start()

    for d in range(1, BLOCKS):
        @pl.when(me >= d)
        def _():
            key_copy(d, (me + d) % n).wait_recv()
            key_share(d, my_rows).start()

        @pl.when(me < d)
        def _():
            key0[BLOCKS - 1 - d] = jnp.zeros((tok, WIDE), jnp.bfloat16)

    for d in range(1, BLOCKS):
        @pl.when(me >= d)
        def _():
            key_share(d, its_rows).wait_recv()

    for b in range(BLOCKS):
        key1[b] = jnp.concatenate(
            [jnp.zeros((tok, ROPE), jnp.bfloat16), key0[b][:, : LAT + ROPE]], axis=-1
        )

    factor = 2.0 / math.sqrt(LAT + ROPE) * math.log2(math.e)
    step = 4

    def attend(parity, keys, g):
        at = pl.ds(g * step, step)
        q = qbuf[parity, at].reshape(step * tok, WIDE)
        s = lax.dot_general(
            q,
            keys[...].reshape(BLOCKS * tok, WIDE),
            (((1,), (1,)), ((), ())),
            preferred_element_type=jnp.float32,
        )
        s = s.reshape(step, tok, BLOCKS * tok) + bias[...][None]
        top = jnp.max(s, axis=-1, keepdims=True)
        e = jnp.exp2((s - top) * factor)
        p = (e * (1.0 / jnp.sum(e, axis=-1, keepdims=True))).astype(jnp.bfloat16)
        out = jnp.dot(
            p.reshape(step * tok, BLOCKS * tok),
            key0[:, :, :LAT].reshape(BLOCKS * tok, LAT),
            preferred_element_type=jnp.float32,
        )
        latent[parity, at] = out.astype(jnp.bfloat16).reshape(step, tok, LAT)

    plan = [
        [lambda: relay(2, True), lambda: relay_x(1)],
        [lambda: relay(2, False)],
        [lambda: relay(3, True), lambda: relay_x(2)],
        [lambda: relay(3, False)],
    ]
    last = [lambda: relay_x(3)]
    for copy in q_copies:
        copy.wait()
    spots = iter(plan)
    for parity, keys in ((0, key0), (1, key1)):
        for lower in (0, 2):
            for event in next(spots):
                event()

            def some(g, carry, parity=parity, keys=keys):
                attend(parity, keys, g)
                return carry

            lax.fori_loop(lower, lower + 2, some, 0)

    group = heads // GROUPS
    wide = group * w_up.shape[2]
    vdim = w_up.shape[2]

    def gcols(g):
        return pl.ds(pl.multiple_of(g * wide, wide), wide)

    def piece_copy(g, k):
        to = (me + k) % n
        return remote(
            send.at[to, :, gcols(g)],
            recv.at[me, :, gcols(g)],
            send_sem.at[g, to],
            recv_sem.at[g, me],
            {"ranks": to},
        )

    def piece_in(g, r):
        return remote(
            send.at[r, :, gcols(g)],
            recv.at[r, :, gcols(g)],
            send_sem.at[g, r],
            recv_sem.at[g, r],
            {"ranks": r},
        )

    def project(g):
        def one(i, carry):
            for parity in range(2):
                h = g * group + 2 * i + parity
                w = wall[:, h].reshape(LAT, vdim)
                out = jnp.dot(
                    latent[parity, g * (group // 2) + i], w, preferred_element_type=jnp.float32
                ).astype(jnp.bfloat16)
                moved = jnp.dot(out_mat[0], out, preferred_element_type=jnp.float32)
                cols = pl.ds(pl.multiple_of(h * vdim, vdim), vdim)
                send[:, :, cols] = moved.astype(jnp.bfloat16).reshape(n, PIECE, vdim)
            return carry

        lax.fori_loop(0, group // 2, one, 0)
        for k in range(1, n):
            piece_copy(g, k).start()
        recv[me, :, gcols(g)] = send[me, :, gcols(g)]

    def c_share(r):
        return remote(crecv.at[r], crecv.at[r], c_share_send.at[r], c_share_recv.at[r], {"tensor": 1 - core})

    def c_sides(side, act):
        for j in range(n // 2):
            r = 2 * j + side

            @pl.when(r != me)
            def _():
                act(r)

    def c_forward(r):
        remote(csend.at[r], crecv.at[r], c_send.at[r], c_recv.at[r], {"ranks": twin}).wait_recv()
        c_share(r).start()

    own_copy.wait()
    gathered(x)
    for i in range(GROUPS // 2):
        project(x * (GROUPS // 2) + i)
    c_sides(core, c_forward)
    for event in last:
        event()
    arrived(twin, 1 - x, False)
    gathered(None)
    for i in range(GROUPS // 2):
        project((1 - x) * (GROUPS // 2) + i)

    c_sides(1 - core, lambda r: c_share(r).wait_recv())
    kept = lax.dot_general(
        crecv[...].reshape(n * PIECE, WIDE),
        in_mat[1],
        (((0,), (1,)), ((), ())),
        preferred_element_type=jnp.float32,
    )
    store[...] = kept[: LAT + ROPE].astype(jnp.bfloat16)
    for i in range(GROUPS):
        g = (x * (GROUPS // 2) + i) % GROUPS
        for k in range(1, n):
            r = (me + k) % n
            piece_in(g, r).wait_recv()
        served[:, gcols(g)] = jnp.dot(
            in_mat[0],
            recv[:, :, gcols(g)].reshape(n * PIECE, wide),
            preferred_element_type=jnp.float32,
        ).astype(jnp.bfloat16)

    y_own(x).wait_send()
    y_own(1 - x).wait_send()
    for d in range(1, BLOCKS):
        @pl.when(me + d < n)
        def _():
            key_copy(d, (me + d) % n).wait_send()

        @pl.when(me >= d)
        def _():
            key_share(d, my_rows).wait_send()

    @pl.when(y == core)
    def _():
        for k in range(1, n):
            c_copy(k).wait_send()

    c_sides(core, lambda r: c_share(r).wait_send())
    for k in range(1, n):
        for g in range(GROUPS):
            piece_copy(g, k).wait_send()
    for level in range(levels):
        for other in (False, True):
            r = 2 * level + (1 - y if other else y)

            @pl.when((z >= level) & (z < levels - 1))
            def _():
                up_hop(r, near(r, x, other), other).wait_send()

            @pl.when((z <= level) & (z > 0))
            def _():
                down_hop(r, near(r, x, other), other).wait_send()

            @pl.when(z != level)
            def _():
                x_hop(r, other).wait_send()
                if not other:
                    y_far(r, x).wait_send()
                    y_far(r, 1 - x).wait_send()


def fused(hidden, w_down, latent_gain, queries, w_up_value, prompt_blocks, migrate, owners):
    n = lax.axis_size("ranks")
    tok, depth = hidden.shape
    heads, _, vdim = w_up_value.shape
    any_space = pl.BlockSpec(memory_space=pl.ANY)
    vmem = pl.BlockSpec(memory_space=pltpu.VMEM)
    bf16 = jnp.bfloat16
    dma = pltpu.SemaphoreType.DMA
    served, store = pl.pallas_call(
        functools.partial(kernel, n),
        out_shape=(
            jax.ShapeDtypeStruct((tok, heads * vdim), bf16),
            jax.ShapeDtypeStruct((LAT + ROPE, tok), bf16),
        ),
        in_specs=[any_space] * 8,
        out_specs=(vmem, vmem),
        scratch_shapes=[
            pltpu.VMEM((tok, depth), bf16),
            pltpu.VMEM((LAT + ROPE, depth), bf16),
            pltpu.VMEM((2, heads // 2, tok, WIDE), bf16),
            pltpu.VMEM((n, heads, w_up_value.shape[1], vdim), bf16),
            pltpu.VMEM((tok, LAT + ROPE), jnp.float32),
            pltpu.VMEM((tok, LAT + ROPE), jnp.float32),
            pltpu.VMEM((BLOCKS, tok, WIDE), bf16),
            pltpu.VMEM((BLOCKS, tok, WIDE), bf16),
            pltpu.VMEM((2, heads // 2, tok, LAT), bf16),
            pltpu.VMEM((tok, BLOCKS * tok), jnp.float32),
            pltpu.VMEM((2, tok, tok), bf16),
            pltpu.VMEM((2, tok, tok), bf16),
            pltpu.VMEM((n, PIECE, heads * vdim), bf16),
            pltpu.VMEM((n, PIECE, heads * vdim), bf16),
            pltpu.VMEM((n, PIECE, WIDE), bf16),
            pltpu.VMEM((n, PIECE, WIDE), bf16),
            pltpu.VMEM((LAT,), bf16),
            pltpu.SMEM(prompt_blocks.shape, jnp.int32),
            pltpu.SMEM(migrate.shape, jnp.int32),
            pltpu.SMEM(owners.shape, jnp.int32),
            dma((4,)),
            dma(()),
            dma((4,)),
            dma((2, heads // 2)),
            dma(()),
            dma((2,)),
            dma((BLOCKS,)),
            dma((BLOCKS,)),
            dma((BLOCKS,)),
            dma((BLOCKS,)),
            dma((n,)),
            dma((n,)),
            dma((n, 2)),
            dma((n,)),
            dma((n,)),
            dma((n,)),
            dma((n, 2, 2)),
            dma((GROUPS, n)),
            dma((GROUPS, n)),
            dma((n,)),
            dma((n,)),
        ],
        compiler_params=pltpu.CompilerParams(
            collective_id=0, has_side_effects=True, vmem_limit_bytes=63 * 1024 * 1024
        ),
    )(
        hidden, w_down.T, latent_gain, queries, w_up_value,
        prompt_blocks, migrate, owners,
    )
    return served, store.T


def solution(mesh):
    sizes = dict(mesh.shape)
    small = sizes["ranks"] == 8 and sizes["groups"] == 2 and sizes["tensor"] == 2
    placed = (
        P(("groups", "ranks"), "tensor"),
        P("tensor", None),
        P(),
        P(("groups", "ranks"), "tensor"),
        P("tensor", "ranks", None),
        P("groups"),
        P("groups", None),
        P("groups", None),
    )
    return jax.shard_map(
        fused if small else body,
        mesh=mesh,
        in_specs=placed,
        out_specs=(P(("groups", "ranks"), "tensor"), P(("groups", "ranks"), None)),
        check_vma=False,
    )
```

```python
import functools
import math

import jax
import jax.numpy as jnp
from jax import lax
from jax.experimental import pallas as pl
from jax.experimental.pallas import tpu as pltpu
from jax.sharding import PartitionSpec as P

LAT = 512
ROPE = 64


def passed_along(block, axis, distance):
    devices = range(lax.axis_size(axis))
    route = [(i - distance, i) for i in devices if i - distance in devices]
    return lax.ppermute(block, axis, route)


def normalize(latent_raw, latent_gain):
    latent_part = latent_raw[:, :LAT]
    mean_square = jnp.mean(latent_part * latent_part, axis=-1, keepdims=True)
    normed = latent_part * lax.rsqrt(mean_square + 1e-06) * latent_gain.astype(jnp.float32)
    return jnp.concatenate([normed, latent_raw[:, LAT:]], axis=-1).astype(jnp.bfloat16)


def block_starts(prompt_blocks, rank_count):
    prompt_ends = jnp.cumsum(prompt_blocks)
    prompt_firsts = prompt_ends - prompt_blocks
    block_ids = jnp.arange(rank_count, dtype=jnp.int32)
    holder = jnp.sum((block_ids[:, None] >= prompt_ends[None, :]).astype(jnp.int32), axis=1)
    return jnp.take(prompt_firsts, holder)


def send_buffer(values, routes, my_rank, rank_count):
    piece_count = routes.shape[1]
    pieces = values.reshape(piece_count, values.shape[0] // piece_count, values.shape[1])
    own_routes = jnp.take(routes, my_rank, axis=0)
    one_hot = (own_routes[None, :] == jnp.arange(rank_count, dtype=jnp.int32)[:, None]).astype(
        jnp.bfloat16
    )
    return jnp.einsum("dp,prc->drc", one_hot, pieces, preferred_element_type=jnp.float32).astype(
        jnp.bfloat16
    )


def pick_slots(received, routes, my_rank):
    selector = (jnp.transpose(routes) == my_rank).astype(jnp.bfloat16)
    placed = jnp.einsum("pr,rqc->pqc", selector, received, preferred_element_type=jnp.float32)
    return placed.astype(jnp.bfloat16).reshape(-1, received.shape[2])


def body(hidden, w_down, latent_gain, queries, w_up_value, prompt_blocks, migrate, owners):
    tok_rows = hidden.shape[0]
    width = LAT + ROPE
    partial_latent = jnp.dot(hidden, w_down, preferred_element_type=jnp.float32)
    summed = lax.psum(partial_latent, "tensor")
    cache_rows = normalize(summed, latent_gain)
    my_rank = lax.axis_index("ranks")
    rank_count = lax.axis_size("ranks")
    span = rank_count // 2
    window = cache_rows[None]
    for level in range(span.bit_length() - 1):
        incoming = passed_along(window, "ranks", 2**level)
        window = jnp.concatenate([incoming, window], axis=0)
    starts = block_starts(prompt_blocks, rank_count)
    first_block = jnp.take(starts, my_rank)
    first_key = first_block * tok_rows
    lowest = jnp.maximum(first_block - my_rank + span - 1, 0)
    query_pos = my_rank * tok_rows + jnp.arange(tok_rows, dtype=jnp.int32)
    local_heads = queries.shape[1] // width
    group_size = 16
    group_count = local_heads // group_size
    grouped = jnp.transpose(queries.reshape(tok_rows, group_count, group_size, width), (1, 0, 2, 3))
    score_scale = 2.0 / math.sqrt(width)

    def attend(query_group):
        empty = jnp.full((group_size, tok_rows, span * tok_rows), -1e30, jnp.float32)

        def fill(block, buffer):
            keys = lax.dynamic_index_in_dim(window, block, 0, keepdims=False)
            scores = (
                jnp.einsum("thd,sd->hts", query_group, keys, preferred_element_type=jnp.float32)
                * score_scale
            )
            key_pos = (my_rank - (span - 1) + block) * tok_rows + jnp.arange(
                tok_rows, dtype=jnp.int32
            )
            allowed = (key_pos[None, :] >= first_key) & (key_pos[None, :] <= query_pos[:, None])
            scores = jnp.where(allowed[None], scores, jnp.float32(-1e30))
            return lax.dynamic_update_slice_in_dim(buffer, scores, block * tok_rows, 2)

        scores = lax.fori_loop(lowest, span, fill, empty)
        highest = jnp.max(scores, axis=-1, keepdims=True)
        expos = jnp.exp(scores - highest)
        probs = (expos / jnp.sum(expos, axis=-1, keepdims=True)).astype(jnp.bfloat16)

        def collect(block, running):
            weights = lax.dynamic_slice_in_dim(probs, block * tok_rows, tok_rows, 2)
            keys = lax.dynamic_index_in_dim(window, block, 0, keepdims=False)[:, :LAT]
            return running + jnp.einsum(
                "hts,sl->thl", weights, keys, preferred_element_type=jnp.float32
            )

        start_out = jnp.zeros((tok_rows, group_size, LAT), jnp.float32)
        return lax.fori_loop(lowest, span, collect, start_out).astype(jnp.bfloat16)

    grouped_out = lax.map(attend, grouped)
    latent_out = jnp.transpose(grouped_out, (1, 0, 2, 3)).reshape(tok_rows, local_heads, LAT)
    summed_values = jnp.einsum(
        "thl,hlv->thv",
        latent_out,
        lax.all_gather(w_up_value, "ranks", axis=1, tiled=True),
        preferred_element_type=jnp.float32,
    )
    head_out = summed_values.astype(jnp.bfloat16).reshape(
        tok_rows, local_heads * w_up_value.shape[2]
    )
    outgoing = send_buffer(head_out, migrate, my_rank, rank_count)
    arrived = lax.all_to_all(outgoing, "ranks", split_axis=0, concat_axis=0, tiled=True)
    served = pick_slots(arrived, migrate, my_rank)
    cache_out = send_buffer(cache_rows, owners, my_rank, rank_count)
    cache_in = lax.all_to_all(cache_out, "ranks", split_axis=0, concat_axis=0, tiled=True)
    cache_store = pick_slots(cache_in, owners, my_rank)
    return (served, cache_store)


PIECE = 16
WIDE = LAT + 2 * ROPE
BLOCKS = 4
GROUPS = 4
MESH = pl.DeviceIdType.MESH


def remote(src, dst, send_sem, recv_sem, where):
    return pltpu.make_async_remote_copy(
        src_ref=src,
        dst_ref=dst,
        send_sem=send_sem,
        recv_sem=recv_sem,
        device_id=where,
        device_id_type=MESH,
    )


def by_piece(index, values):
    out = jnp.zeros_like(index)
    for p, value in enumerate(values):
        out = jnp.where((index // PIECE) == p, value, out)
    return out


def send_matrix(routes, me, n):
    rows = lax.broadcasted_iota(jnp.int32, (n * PIECE, n * PIECE), 0)
    cols = lax.broadcasted_iota(jnp.int32, (n * PIECE, n * PIECE), 1)
    target = by_piece(cols, [routes[me, p] for p in range(n)])
    hit = ((rows // PIECE) == target) & ((rows % PIECE) == (cols % PIECE))
    return jnp.where(hit, 1.0, 0.0).astype(jnp.bfloat16)


def take_matrix(routes, me, n):
    rows = lax.broadcasted_iota(jnp.int32, (n * PIECE, n * PIECE), 0)
    cols = lax.broadcasted_iota(jnp.int32, (n * PIECE, n * PIECE), 1)
    origins = []
    for p in range(n):
        origin = jnp.int32(0)
        for r in range(n):
            origin = origin + jnp.where(routes[r, p] == me, r, 0)
        origins.append(origin)
    source = by_piece(rows, origins)
    hit = ((cols // PIECE) == source) & ((rows % PIECE) == (cols % PIECE))
    return jnp.where(hit, 1.0, 0.0).astype(jnp.bfloat16)


def kernel(
    n, hidden, w_down, gain_in, queries, w_up, blocks_in, migrate_in, owners_in,
    served, store,
    hid, wd, qbuf, wall, part, part_in, key0, key1, latent, bias, out_mat, in_mat,
    send, recv, csend, crecv,
    gain, prompt_blocks, migrate, owners, small_sem,
    hid_sem, wd_sem, q_sem, own_sem, part_sem, key_send, key_recv,
    share_send, share_recv, c_share_send, c_share_recv,
    y_send, up_send, down_send, x_send, w_recv, send_sem, recv_sem, c_send, c_recv,
):
    me = lax.axis_index("ranks")
    x = lax.axis_index("groups")
    core = lax.axis_index("tensor")
    z, y = me // 2, me % 2
    levels = n // 2
    tok = hid.shape[0]
    heads = w_up.shape[0]
    half = heads // 2
    pairs = heads // 2
    twin = 2 * z + (1 - y)
    other_x = {"groups": 1 - x}

    chunks = wd_sem.shape[0]
    rows = wd.shape[1] // chunks
    hid_copy = pltpu.make_async_copy(hidden, hid, hid_sem)
    hid_copy.start()
    wd_copies = []
    for c in range(chunks):
        cut = pl.ds(c * rows, rows)
        wd_copies.append(
            pltpu.make_async_copy(w_down.at[:, cut], wd.at[:, cut], wd_sem.at[c])
        )
        wd_copies[-1].start()

    small = [
        pltpu.make_async_copy(src, dst, small_sem.at[i])
        for i, (src, dst) in enumerate(
            ((gain_in, gain), (blocks_in, prompt_blocks), (migrate_in, migrate), (owners_in, owners))
        )
    ]
    for copy in small:
        copy.start()

    barrier = pltpu.get_barrier_semaphore()
    for k in range(1, n):
        pl.semaphore_signal(barrier, 1, device_id={"ranks": (me + k) % n}, device_id_type=MESH)
    pl.semaphore_signal(barrier, 1, device_id={"tensor": 1 - core}, device_id_type=MESH)
    pl.semaphore_signal(barrier, 1, device_id=other_x, device_id_type=MESH)
    pl.semaphore_wait(barrier, n + 1)

    quarter = half // 2

    def near(r, h, other):
        return wall.at[r, pl.ds(h * half, quarter if other else half)]

    def far(r, h):
        return wall.at[r, pl.ds(h * half + quarter, quarter)]

    def own(h, other):
        return w_up.at[pl.ds(h * half, quarter if other else half)]

    def y_own(h):
        return remote(own(h, False), near(me, h, False), y_send.at[me, h], w_recv.at[me, h, 0], {"ranks": twin})

    def y_far(r, h):
        return remote(far(r, h), far(r, h), y_send.at[r, h], w_recv.at[r, h, 1], {"ranks": twin})

    def up_hop(r, src, other):
        to = {"ranks": jnp.minimum(me + 2, n - 2 + y)}
        return remote(src, near(r, x, other), up_send.at[r], w_recv.at[r, x, 0], to)

    def down_hop(r, src, other):
        to = {"ranks": jnp.maximum(me - 2, y)}
        return remote(src, near(r, x, other), down_send.at[r], w_recv.at[r, x, 0], to)

    def x_hop(r, other):
        return remote(near(r, x, other), near(r, x, other), x_send.at[r], w_recv.at[r, x, 0], other_x)

    def arrived(r, h, other):
        remote(near(r, h, other), near(r, h, other), x_send.at[r], w_recv.at[r, h, 0], other_x).wait_recv()

    own_copy = pltpu.make_async_copy(w_up, wall.at[me], own_sem)

    def at_levels(d, other, act):
        for sign, within in ((-1, z >= d), (1, z + d < levels)):
            @pl.when(within)
            def _():
                level = jnp.clip(z + sign * d, 0, levels - 1)
                act(2 * level + (1 - y if other else y), sign)

    def relay(d, same):
        other = not same

        def act(r, sign):
            arrived(r, x, other)
            if d < levels - 1:
                if sign < 0:
                    @pl.when(z < levels - 1)
                    def _():
                        up_hop(r, near(r, x, other), other).start()
                else:
                    @pl.when(z > 0)
                    def _():
                        down_hop(r, near(r, x, other), other).start()

            x_hop(r, other).start()
            if same:
                y_far(r, x).start()

        at_levels(d, other, act)

    def relay_x(d):
        def act(r, sign):
            arrived(r, 1 - x, False)
            y_far(r, 1 - x).start()

        at_levels(d, False, act)

    def gathered(h):
        def act(r, sign):
            y_far(r, h).wait_recv()

        for d in range(1, levels):
            at_levels(d, True, act)

    y_own(x).start()

    @pl.when(z < levels - 1)
    def _():
        up_hop(me, own(x, False), False).start()

    @pl.when(z > 0)
    def _():
        down_hop(me, own(x, False), False).start()

    q_copies = []
    for parity in range(2):
        for i in range(pairs):
            q_copies.append(
                pltpu.make_async_copy(
                    queries.at[:, pl.ds(i * 2 * (LAT + ROPE) + parity * LAT, WIDE)],
                    qbuf.at[parity, i],
                    q_sem.at[parity, i],
                )
            )
            q_copies[-1].start()
    own_copy.start()
    y_own(1 - x).start()

    hid_copy.wait()
    for c in range(chunks):
        wd_copies[c].wait()
        term = lax.dot_general(
            hid[:, c * rows : (c + 1) * rows],
            wd[:, c * rows : (c + 1) * rows],
            (((1,), (1,)), ((), ())),
            preferred_element_type=jnp.float32,
        )
        part[...] = term if c == 0 else part[...] + term
    part_copy = remote(part, part_in, part_sem.at[0], part_sem.at[1], {"tensor": 1 - core})
    part_copy.start()

    arrived(twin, x, False)

    @pl.when(z < levels - 1)
    def _():
        up_hop(twin, near(twin, x, True), True).start()

    @pl.when(z > 0)
    def _():
        down_hop(twin, near(twin, x, True), True).start()

    relay(1, True)
    for copy in small:
        copy.wait()
    out_mat[0] = send_matrix(migrate, me, n)
    out_mat[1] = send_matrix(owners, me, n)
    in_mat[0] = take_matrix(migrate, me, n)
    in_mat[1] = take_matrix(owners, me, n)
    first = jnp.int32(0)
    end = jnp.int32(0)
    for i in range(prompt_blocks.shape[0]):
        end = end + prompt_blocks[i]
        first = jnp.where(me >= end, end, first)
    query_pos = me * tok + lax.broadcasted_iota(jnp.int32, (tok, BLOCKS * tok), 0)
    key_pos = (me - (BLOCKS - 1)) * tok + lax.broadcasted_iota(jnp.int32, (tok, BLOCKS * tok), 1)
    allowed = (key_pos >= first * tok) & (key_pos <= query_pos)
    bias[...] = jnp.where(allowed, 0.0, -1e30)

    part_copy.wait()
    raw = part[...] + part_in[...]
    lead = raw[:, :LAT]
    mean_square = jnp.mean(lead * lead, axis=-1, keepdims=True)
    normed = lead * lax.rsqrt(mean_square + 1e-06) * gain[...].astype(jnp.float32).reshape(1, LAT)
    rope = raw[:, LAT:]
    blank = jnp.zeros((tok, ROPE), jnp.float32)
    key0[BLOCKS - 1] = jnp.concatenate([normed, rope, blank], axis=-1).astype(jnp.bfloat16)

    my_rows = pl.ds(core * (tok // 2), tok // 2)
    its_rows = pl.ds((1 - core) * (tok // 2), tok // 2)

    def key_copy(d, r):
        return remote(
            key0.at[BLOCKS - 1, my_rows],
            key0.at[BLOCKS - 1 - d, my_rows],
            key_send.at[d],
            key_recv.at[d],
            {"ranks": r},
        )

    def key_share(d, part_rows):
        block = key0.at[BLOCKS - 1 - d, part_rows]
        return remote(block, block, share_send.at[d], share_recv.at[d], {"tensor": 1 - core})

    for d in range(1, BLOCKS):
        @pl.when(me + d < n)
        def _():
            key_copy(d, (me + d) % n).start()

    relay(1, False)
    csend[...] = (
        jnp.dot(out_mat[1], key0[BLOCKS - 1], preferred_element_type=jnp.float32)
        .astype(jnp.bfloat16)
        .reshape(n, PIECE, WIDE)
    )
    crecv[me] = csend[me]

    def c_copy(k):
        to = (me + k) % n
        return remote(csend.at[to], crecv.at[me], c_send.at[to], c_recv.at[me], {"ranks": to})

    for d in range(1, BLOCKS):
        @pl.when(me >= d)
        def _():
            key_copy(d, (me + d) % n).wait_recv()
            key_share(d, my_rows).start()

        @pl.when(me < d)
        def _():
            key0[BLOCKS - 1 - d] = jnp.zeros((tok, WIDE), jnp.bfloat16)

    for d in range(1, BLOCKS):
        @pl.when(me >= d)
        def _():
            key_share(d, its_rows).wait_recv()

    for b in range(BLOCKS):
        key1[b] = jnp.concatenate(
            [jnp.zeros((tok, ROPE), jnp.bfloat16), key0[b][:, : LAT + ROPE]], axis=-1
        )

    factor = 2.0 / math.sqrt(LAT + ROPE) * math.log2(math.e)
    step = 4

    def attend(parity, keys, g):
        at = pl.ds(g * step, step)
        q = qbuf[parity, at].reshape(step * tok, WIDE)
        s = lax.dot_general(
            q,
            keys[...].reshape(BLOCKS * tok, WIDE),
            (((1,), (1,)), ((), ())),
            preferred_element_type=jnp.float32,
        )
        s = s.reshape(step, tok, BLOCKS * tok) + bias[...][None]
        top = jnp.max(s, axis=-1, keepdims=True)
        e = jnp.exp2((s - top) * factor)
        p = (e * (1.0 / jnp.sum(e, axis=-1, keepdims=True))).astype(jnp.bfloat16)
        out = jnp.dot(
            p.reshape(step * tok, BLOCKS * tok),
            key0[:, :, :LAT].reshape(BLOCKS * tok, LAT),
            preferred_element_type=jnp.float32,
        )
        latent[parity, at] = out.astype(jnp.bfloat16).reshape(step, tok, LAT)

    plan = [
        [lambda: relay(2, True)],
        [lambda: relay_x(1), lambda: relay(2, False)],
        [lambda: relay(3, True)],
        [lambda: relay_x(2)],
    ]
    last = [lambda: relay_x(3)]
    for copy in q_copies:
        copy.wait()
    spots = iter(plan)
    for parity, keys in ((0, key0), (1, key1)):
        for lower in (0, 2):
            for event in next(spots):
                event()

            def some(g, carry, parity=parity, keys=keys):
                attend(parity, keys, g)
                return carry

            lax.fori_loop(lower, lower + 2, some, 0)

    group = heads // GROUPS
    wide = group * w_up.shape[2]
    vdim = w_up.shape[2]

    def gcols(g):
        return pl.ds(pl.multiple_of(g * wide, wide), wide)

    def piece_copy(g, k):
        to = (me + k) % n
        return remote(
            send.at[to, :, gcols(g)],
            recv.at[me, :, gcols(g)],
            send_sem.at[g, to],
            recv_sem.at[g, me],
            {"ranks": to},
        )

    def piece_in(g, r):
        return remote(
            send.at[r, :, gcols(g)],
            recv.at[r, :, gcols(g)],
            send_sem.at[g, r],
            recv_sem.at[g, r],
            {"ranks": r},
        )

    def project(g):
        def one(i, carry):
            for parity in range(2):
                h = g * group + 2 * i + parity
                w = wall[:, h].reshape(LAT, vdim)
                out = jnp.dot(
                    latent[parity, g * (group // 2) + i], w, preferred_element_type=jnp.float32
                ).astype(jnp.bfloat16)
                moved = jnp.dot(out_mat[0], out, preferred_element_type=jnp.float32)
                cols = pl.ds(pl.multiple_of(h * vdim, vdim), vdim)
                send[:, :, cols] = moved.astype(jnp.bfloat16).reshape(n, PIECE, vdim)
            return carry

        lax.fori_loop(0, group // 2, one, 0)
        for k in range(1, n):
            piece_copy(g, k).start()
        recv[me, :, gcols(g)] = send[me, :, gcols(g)]

    def c_share(r):
        return remote(crecv.at[r], crecv.at[r], c_share_send.at[r], c_share_recv.at[r], {"tensor": 1 - core})

    def c_sides(side, act):
        for j in range(n // 2):
            r = 2 * j + side

            @pl.when(r != me)
            def _():
                act(r)

    def c_forward(r):
        remote(csend.at[r], crecv.at[r], c_send.at[r], c_recv.at[r], {"ranks": twin}).wait_recv()
        c_share(r).start()

    @pl.when(y == core)
    def _():
        for k in range(1, n):
            c_copy(k).start()

    own_copy.wait()
    relay(3, False)
    project(2 * x)
    for event in last:
        event()
    gathered(x)
    project(2 * x + 1)
    arrived(twin, 1 - x, False)
    for d in range(1, levels):
        at_levels(d, True, lambda r, sign: arrived(r, 1 - x, True))
    project(2 * (1 - x))
    gathered(1 - x)
    project(2 * (1 - x) + 1)
    c_sides(core, c_forward)

    c_sides(1 - core, lambda r: c_share(r).wait_recv())
    kept = lax.dot_general(
        crecv[...].reshape(n * PIECE, WIDE),
        in_mat[1],
        (((0,), (1,)), ((), ())),
        preferred_element_type=jnp.float32,
    )
    store[...] = kept[: LAT + ROPE].astype(jnp.bfloat16)
    for i in range(GROUPS):
        g = (x * (GROUPS // 2) + i) % GROUPS
        for k in range(1, n):
            r = (me + k) % n
            piece_in(g, r).wait_recv()
        served[:, gcols(g)] = jnp.dot(
            in_mat[0],
            recv[:, :, gcols(g)].reshape(n * PIECE, wide),
            preferred_element_type=jnp.float32,
        ).astype(jnp.bfloat16)

    y_own(x).wait_send()
    y_own(1 - x).wait_send()
    for d in range(1, BLOCKS):
        @pl.when(me + d < n)
        def _():
            key_copy(d, (me + d) % n).wait_send()

        @pl.when(me >= d)
        def _():
            key_share(d, my_rows).wait_send()

    @pl.when(y == core)
    def _():
        for k in range(1, n):
            c_copy(k).wait_send()

    c_sides(core, lambda r: c_share(r).wait_send())
    for k in range(1, n):
        for g in range(GROUPS):
            piece_copy(g, k).wait_send()
    for level in range(levels):
        for other in (False, True):
            r = 2 * level + (1 - y if other else y)

            @pl.when((z >= level) & (z < levels - 1))
            def _():
                up_hop(r, near(r, x, other), other).wait_send()

            @pl.when((z <= level) & (z > 0))
            def _():
                down_hop(r, near(r, x, other), other).wait_send()

            @pl.when(z != level)
            def _():
                x_hop(r, other).wait_send()
                if not other:
                    y_far(r, x).wait_send()
                    y_far(r, 1 - x).wait_send()


def fused(hidden, w_down, latent_gain, queries, w_up_value, prompt_blocks, migrate, owners):
    n = lax.axis_size("ranks")
    tok, depth = hidden.shape
    heads, _, vdim = w_up_value.shape
    any_space = pl.BlockSpec(memory_space=pl.ANY)
    vmem = pl.BlockSpec(memory_space=pltpu.VMEM)
    bf16 = jnp.bfloat16
    dma = pltpu.SemaphoreType.DMA
    served, store = pl.pallas_call(
        functools.partial(kernel, n),
        out_shape=(
            jax.ShapeDtypeStruct((tok, heads * vdim), bf16),
            jax.ShapeDtypeStruct((LAT + ROPE, tok), bf16),
        ),
        in_specs=[any_space] * 8,
        out_specs=(vmem, vmem),
        scratch_shapes=[
            pltpu.VMEM((tok, depth), bf16),
            pltpu.VMEM((LAT + ROPE, depth), bf16),
            pltpu.VMEM((2, heads // 2, tok, WIDE), bf16),
            pltpu.VMEM((n, heads, w_up_value.shape[1], vdim), bf16),
            pltpu.VMEM((tok, LAT + ROPE), jnp.float32),
            pltpu.VMEM((tok, LAT + ROPE), jnp.float32),
            pltpu.VMEM((BLOCKS, tok, WIDE), bf16),
            pltpu.VMEM((BLOCKS, tok, WIDE), bf16),
            pltpu.VMEM((2, heads // 2, tok, LAT), bf16),
            pltpu.VMEM((tok, BLOCKS * tok), jnp.float32),
            pltpu.VMEM((2, tok, tok), bf16),
            pltpu.VMEM((2, tok, tok), bf16),
            pltpu.VMEM((n, PIECE, heads * vdim), bf16),
            pltpu.VMEM((n, PIECE, heads * vdim), bf16),
            pltpu.VMEM((n, PIECE, WIDE), bf16),
            pltpu.VMEM((n, PIECE, WIDE), bf16),
            pltpu.VMEM((LAT,), bf16),
            pltpu.SMEM(prompt_blocks.shape, jnp.int32),
            pltpu.SMEM(migrate.shape, jnp.int32),
            pltpu.SMEM(owners.shape, jnp.int32),
            dma((4,)),
            dma(()),
            dma((4,)),
            dma((2, heads // 2)),
            dma(()),
            dma((2,)),
            dma((BLOCKS,)),
            dma((BLOCKS,)),
            dma((BLOCKS,)),
            dma((BLOCKS,)),
            dma((n,)),
            dma((n,)),
            dma((n, 2)),
            dma((n,)),
            dma((n,)),
            dma((n,)),
            dma((n, 2, 2)),
            dma((GROUPS, n)),
            dma((GROUPS, n)),
            dma((n,)),
            dma((n,)),
        ],
        compiler_params=pltpu.CompilerParams(
            collective_id=0, has_side_effects=True, vmem_limit_bytes=63 * 1024 * 1024
        ),
    )(
        hidden, w_down.T, latent_gain, queries, w_up_value,
        prompt_blocks, migrate, owners,
    )
    return served, store.T


def solution(mesh):
    sizes = dict(mesh.shape)
    small = sizes["ranks"] == 8 and sizes["groups"] == 2 and sizes["tensor"] == 2
    placed = (
        P(("groups", "ranks"), "tensor"),
        P("tensor", None),
        P(),
        P(("groups", "ranks"), "tensor"),
        P("tensor", "ranks", None),
        P("groups"),
        P("groups", None),
        P("groups", None),
    )
    return jax.shard_map(
        fused if small else body,
        mesh=mesh,
        in_specs=placed,
        out_specs=(P(("groups", "ranks"), "tensor"), P(("groups", "ranks"), None)),
        check_vma=False,
    )
```
